32 devices in a mesh: dp: 4 (over z), expert: 8 (over y, x, core).
Axes of the slice: x: 2, y: 2, z: 4, core: 2. Of those that a mesh axis runs over, the one named last changes fastest.
Arguments:
- tokens: bfloat16 [8192, 2048], P(('dp', 'expert')), may hold values from -6 to 6
- expert_ids: int32 [8192, 4], P(('dp', 'expert')), may hold values from 0 to 7, as said below
- gates: float32 [8192, 4], P(('dp', 'expert')), may hold values from 0.1 to 1
- w_gate: bfloat16 [8, 2048, 384], P('expert'), may hold values from -0.125 to 0.125
- w_up: bfloat16 [8, 2048, 384], P('expert'), may hold values from -0.125 to 0.125
- w_down: bfloat16 [8, 2048, 384], P('expert'), may hold values from -0.3125 to 0.3125
- cotangent: bfloat16 [8192, 2048], P(('dp', 'expert')), may hold values from -6 to 6
Outputs:
- mixed: bfloat16 [8192, 2048], P(('dp', 'expert'))
- tokens_grad: bfloat16 [8192, 2048], P(('dp', 'expert'))
- gates_grad: float32 [8192, 4], P(('dp', 'expert'))
- gate_grad: float32 [8, 2048, 384], P('expert', 'dp')
- up_grad: float32 [8, 2048, 384], P('expert', 'dp')
- down_grad: float32 [8, 2048, 384], P('expert', 'dp')
The draws below stay inside these ranges and needn't reach their ends.
Inputs may be any that keep to these rules, and one draw needn't show every extreme that they name: `expert_ids`: each row holds 4 different experts. One expert, the same in every draw position, is named by every token. Among the 256 tokens of one device every other expert is named at most 110 times, and one of them is named exactly 110 times on every device.
All inputs are finite; a program needn't handle non-finite values.
Results may differ from the reference program's by a relative error of at most 0.014.
Values may be sent and summed in bfloat16 or wider, within the bound.
No kernel may reach another device: no remote copies, remote signals or barrier semaphores. Data moves between devices by JAX's collectives and lax.ppermute only.
A program may use at most 128 MiB of HBM per device.

```python
import math
import jax
import jax.numpy as jnp
from jax import lax

D = 2048
FF = 384
TOPK = 4
TOK_DEV = 256
EXPERTS = 8
TOKENS = 8192


def draw_expert_ids(key, part):
    cold_count = EXPERTS - 1
    spread = TOK_DEV * (TOPK - 1)
    surplus = max(spread % cold_count, 1)
    hot_id = jax.random.randint(jax.random.fold_in(key, 101), (), 0, EXPERTS).astype(jnp.int32)
    base_id = jax.random.randint(jax.random.fold_in(key, 102), (), 0, cold_count).astype(jnp.int32)
    block_keys = jax.random.split(jax.random.fold_in(key, 103), TOKENS // TOK_DEV)

    def one_block(block_key):
        perm_key, shift_key, order_key = jax.random.split(block_key, 3)
        ranking = jax.random.permutation(perm_key, TOK_DEV).astype(jnp.int32)
        offset = base_id - jax.random.randint(shift_key, (), 0, surplus).astype(jnp.int32)
        slot_index = ranking[:, None] * (TOPK - 1) + jnp.arange(TOPK - 1, dtype=jnp.int32)[None, :]
        cold_ids = (slot_index + offset) % cold_count
        cold_ids = cold_ids + (cold_ids >= hot_id).astype(jnp.int32)
        chosen = jnp.concatenate([jnp.full((TOK_DEV, 1), hot_id, jnp.int32), cold_ids.astype(jnp.int32)], axis=1)
        scores = jax.random.randint(order_key, (TOK_DEV, TOPK), 0, 1 << 20).astype(jnp.int32) * TOPK + jnp.arange(TOPK, dtype=jnp.int32)[None, :]
        ordering = jnp.argsort(scores, axis=1)
        return jnp.take_along_axis(chosen, ordering, axis=1)
    return lax.map(one_block, block_keys).reshape(TOKENS, TOPK).astype(jnp.int32)


def levels(key, shape, shards, least, top_value):
    factor_of = 1.0
    for axis_at, shards_of in shards:
        heights = jax.random.uniform(jax.random.fold_in(jax.random.fold_in(key, 6), axis_at), (shards_of,), jnp.float32, least / len(shards), top_value / len(shards))
        factor_of = factor_of * jnp.repeat(jnp.exp(heights), shape[axis_at] // shards_of).reshape((-1,) + (1,) * (len(shape) - 1 - axis_at))
    return factor_of


def noise(own_key, dims, deviation, limit, pieces=(), held_as=jnp.bfloat16):
    array = jax.random.normal(own_key, dims, jnp.float32) * deviation
    if len(pieces) > 0:
        array = levels(own_key, dims, pieces, -0.22, 0.18) * array
    return jnp.clip(array, min=-limit, max=limit).astype(held_as)


def setup_inputs(seed: int = 0) -> dict:
    arg_keys = jax.random.split(jax.random.key(seed), 8)
    return {
        "tokens": noise(arg_keys[0], (TOKENS, D), 1.0, 6.0, ((0, 32),)),
        "expert_ids": draw_expert_ids(jax.random.fold_in(arg_keys[7], 71), 0),
        "gates": jnp.clip(jnp.exp(math.log(1.0) - 2.3025851 * jax.random.uniform(arg_keys[2], (TOKENS, TOPK), jnp.float32) ** levels(arg_keys[2], (TOKENS, TOPK), ((0, 32),), -0.2, 0.2)), 0.1, 1.0),
        "w_gate": noise(arg_keys[3], (EXPERTS, D, FF), D ** -0.5, 0.125, ((0, 8),)),
        "w_up": noise(arg_keys[4], (EXPERTS, D, FF), D ** -0.5, 0.125, ((0, 8),)),
        "w_down": noise(arg_keys[5], (EXPERTS, D, FF), FF ** -0.5, 0.3125, ((0, 8),)),
        "cotangent": noise(arg_keys[6], (TOKENS, D), 1.0, 6.0, ((0, 32),)),
    }


def expert_forward(rows, weight_gate, weight_up, weight_down):
    gate_act = jnp.dot(rows, weight_gate, preferred_element_type=jnp.float32)
    up_act = jnp.dot(rows, weight_up, preferred_element_type=jnp.float32)
    hidden = (jax.nn.silu(gate_act) * up_act).astype(jnp.bfloat16)
    output = lax.dot_general(hidden, weight_down, (((1,), (1,)), ((), ())), preferred_element_type=jnp.float32).astype(jnp.bfloat16)
    return gate_act, up_act, hidden, output


def expert_backward(rows, upstream, weight_gate, weight_up, weight_down, gate_act, up_act, hidden):
    hidden_grad = jnp.dot(upstream, weight_down, preferred_element_type=jnp.float32)
    sigma = jax.nn.sigmoid(gate_act)
    gate_pre = (hidden_grad * up_act * sigma * (1.0 + gate_act * (1.0 - sigma))).astype(jnp.bfloat16)
    up_pre = (hidden_grad * gate_act * sigma).astype(jnp.bfloat16)
    contract = (((1,), (1,)), ((), ()))
    input_part = (lax.dot_general(gate_pre, weight_gate, contract, preferred_element_type=jnp.float32)
                  + lax.dot_general(up_pre, weight_up, contract, preferred_element_type=jnp.float32)).astype(jnp.bfloat16)
    over_rows = (((0,), (0,)), ((), ()))
    grad_gate = lax.dot_general(rows, gate_pre, over_rows, preferred_element_type=jnp.float32)
    grad_upper = lax.dot_general(rows, up_pre, over_rows, preferred_element_type=jnp.float32)
    grad_down = lax.dot_general(upstream, hidden, over_rows, preferred_element_type=jnp.float32)
    return input_part, grad_gate, grad_upper, grad_down


def reference(tokens, expert_ids, gates, w_gate, w_up, w_down, cotangent):
    rows_all = TOKENS * TOPK
    block = min(512, rows_all)
    flat_ids = expert_ids.reshape(-1)
    ordering = jnp.argsort(flat_ids, stable=True).astype(jnp.int32)
    sorted_ids = flat_ids[ordering]
    sorted_gates = gates.reshape(-1)[ordering]
    block_count = rows_all // block

    def one_block(carry, block_index):
        mixed, tokens_grad, grad_g, grad_u, grad_d = carry
        start = (block_index * block).astype(jnp.int32)
        picked = lax.dynamic_slice_in_dim(ordering, start, block)
        ids_here = lax.dynamic_slice_in_dim(sorted_ids, start, block)
        gate_here = lax.dynamic_slice_in_dim(sorted_gates, start, block)
        token_index = (picked // TOPK).astype(jnp.int32)
        rows = tokens[token_index]
        upstream = cotangent[token_index]
        slot_grad = (gate_here[:, None] * upstream.astype(jnp.float32)).astype(jnp.bfloat16)

        def per_expert(expert, inner):
            out_sum, input_sum, grad_g, grad_u, grad_d = inner
            selected = (ids_here == expert)[:, None]
            xin = jnp.where(selected, rows, jnp.zeros_like(rows))
            din = jnp.where(selected, slot_grad, jnp.zeros_like(slot_grad))
            weight_gate = lax.dynamic_index_in_dim(w_gate, expert, 0, keepdims=False)
            weight_up = lax.dynamic_index_in_dim(w_up, expert, 0, keepdims=False)
            weight_down = lax.dynamic_index_in_dim(w_down, expert, 0, keepdims=False)
            gate_act, up_act, hidden, output = expert_forward(xin, weight_gate, weight_up, weight_down)
            input_part, grad_gate, grad_upper, grad_down = expert_backward(xin, din, weight_gate, weight_up, weight_down, gate_act, up_act, hidden)
            out_sum = out_sum + output.astype(jnp.float32)
            input_sum = input_sum + input_part.astype(jnp.float32)
            grad_g = grad_g.at[expert].add(grad_gate)
            grad_u = grad_u.at[expert].add(grad_upper)
            grad_d = grad_d.at[expert].add(grad_down)
            return out_sum, input_sum, grad_g, grad_u, grad_d

        zero_rows = jnp.zeros((block, D), jnp.float32)
        out_sum, input_sum, grad_g, grad_u, grad_d = lax.fori_loop(
            ids_here[0], ids_here[block - 1] + 1, per_expert, (zero_rows, zero_rows, grad_g, grad_u, grad_d))
        dgate_here = jnp.sum(upstream.astype(jnp.float32) * out_sum, axis=1)
        mixed = mixed.at[token_index].add(gate_here[:, None] * out_sum)
        tokens_grad = tokens_grad.at[token_index].add(input_sum)
        return (mixed, tokens_grad, grad_g, grad_u, grad_d), dgate_here

    zero_tokens = jnp.zeros((TOKENS, D), jnp.float32)
    zero_weights = jnp.zeros((EXPERTS, D, FF), jnp.float32)
    final, dgates_sorted = lax.scan(one_block, (zero_tokens, zero_tokens, zero_weights, zero_weights, zero_weights),
                                    jnp.arange(block_count, dtype=jnp.int32))
    mixed, tokens_grad, grad_g, grad_u, grad_d = final
    gates_grad = jnp.zeros((rows_all,), jnp.float32).at[ordering].set(dgates_sorted.reshape(-1)).reshape(TOKENS, TOPK)
    return (mixed.astype(jnp.bfloat16), tokens_grad.astype(jnp.bfloat16), gates_grad, grad_g, grad_u, grad_d)
```

```python
import jax
import jax.numpy as jnp
from jax import lax
from jax.experimental import pallas as pl
from jax.experimental.pallas import tpu as pltpu
from jax.sharding import PartitionSpec as P

BF = jnp.bfloat16
F32 = jnp.float32
OVER_ROWS = (((0,), (0,)), ((), ()))
OVER_COLS = (((1,), (1,)), ((), ()))


def add(left, right):
    return (left.astype(F32) + right.astype(F32)).astype(BF)


def join(*values):
    return jnp.concatenate(values, axis=0)


def ends_round(*values):
    return lax.optimization_barrier(values)


def chip_bits():
    return [1 << b for b in range(1, lax.axis_size("expert").bit_length() - 1)]


def flip(value, bit_even, bit_odd):
    size = lax.axis_size("expert")
    pairs = [(i, i ^ (bit_odd if i & 1 else bit_even)) for i in range(size)]
    return lax.ppermute(value, "expert", pairs)


def swap_core(value):
    return flip(value, 1, 1)


def hop(value, step):
    bits = chip_bits()
    return flip(value, bits[step], bits[-1 - step])


def take(stacked, index):
    return lax.dynamic_index_in_dim(stacked, index, 0, keepdims=False)


class LineSum:
    def __init__(self, part):
        self.part = part
        self.size = lax.axis_size("dp")
        self.right, self.left = None, None

    def block(self, index):
        width = self.part.shape[1] // self.size
        start = jnp.clip(index, 0, self.size - 1) * width
        return lax.dynamic_slice_in_dim(self.part, start, width, 1)

    def sends(self, step):
        size, me = self.size, lax.axis_index("dp")
        right, left = self.block(size - step + me), self.block(me - (size - step))
        if step > 1:
            right, left = add(right, self.right), add(left, self.left)
        return right, left

    def send(self, step, right, left):
        size = self.size
        self.right = lax.ppermute(right, "dp", [(i, i + 1) for i in range(step)])
        self.left = lax.ppermute(left, "dp", [(size - 1 - i, size - 2 - i) for i in range(step)])

def line_gather(mine):
    groups = lax.axis_size("dp")
    group = lax.axis_index("dp")
    found = mine[None]
    bit = 1
    while bit < groups:
        found = join(found, lax.ppermute(found, "dp", [(i, i ^ bit) for i in range(groups)]))
        bit *= 2
    return jnp.concatenate([take(found, group ^ j) for j in range(groups)], axis=1)


def row_order():
    lists = []
    for bits in (chip_bits(), chip_bits()[::-1]):
        held = [0]
        for bit in bits:
            held = held + [r ^ bit for r in held]
        lists.append(held)
    half = len(lists[0]) // 2
    orders = []
    for core in (0, 1):
        own, other = lists[core], [r ^ 1 for r in lists[1 - core]]
        orders.append(own[:half] + other[:half] + own[half:] + other[half:])
    return orders


def tile_of(rows):
    tile = min(rows, 256)
    assert rows % tile == 0
    return tile


def call(body, grid, in_specs, out_specs, out_shape):
    return pl.pallas_call(
        body,
        grid=grid,
        in_specs=in_specs,
        out_specs=out_specs,
        out_shape=out_shape,
        cost_estimate=pl.CostEstimate(flops=1000, bytes_accessed=1000, transcendentals=0),
        compiler_params=pltpu.CompilerParams(
            dimension_semantics=("arbitrary",), vmem_limit_bytes=48 * 1024 * 1024
        ),
    )


def by_rows(tile, width):
    return pl.BlockSpec((tile, width), lambda i: (i, 0))


def by_columns(height, tile):
    return pl.BlockSpec((height, tile), lambda i: (0, i))


def whole(shape):
    return pl.BlockSpec(shape, lambda i: (0, 0))


def row_weights(gate_ref, units, shape):
    lane = lax.broadcasted_iota(jnp.int32, shape, 1)
    return jnp.where(lane < units, gate_ref[:, 0:1], gate_ref[:, 1:2])


def first_rows(tile, width, tiles):
    return pl.BlockSpec((tile, width), lambda i: (jnp.minimum(i, tiles - 1), 0))


def second_rows(tile, width, tiles):
    return pl.BlockSpec((tile, width), lambda i: (jnp.maximum(i - tiles, 0), 0))


def on_both(tiles, run, first, second):
    pl.when(pl.program_id(0) < tiles)(lambda: run(*first))
    pl.when(pl.program_id(0) >= tiles)(lambda: run(*second))


def forward(first, second, gate, w_in, w_out, units):
    half, width = first.shape
    count = 2 * half
    hidden_width = w_out.shape[1]
    tile = tile_of(half)
    tiles = half // tile

    def body(a_ref, b_ref, g_ref, wi_ref, wo_ref, act_ref, hidden_ref, out_a_ref, out_b_ref):
        def run(x_ref, out_ref):
            act = jnp.dot(x_ref[...], wi_ref[...], preferred_element_type=F32)
            act_ref[...] = act
            gate_act, up_act = act[:, :hidden_width], act[:, hidden_width:]
            weight = row_weights(g_ref, units, gate_act.shape)
            hidden = (gate_act * jax.nn.sigmoid(gate_act) * up_act * weight).astype(BF)
            hidden_ref[...] = hidden.T
            out_ref[...] = lax.dot_general(
                hidden, wo_ref[...], OVER_COLS, preferred_element_type=F32
            ).astype(BF)

        on_both(tiles, run, (a_ref, out_a_ref), (b_ref, out_b_ref))

    return call(
        body,
        (2 * tiles,),
        [
            first_rows(tile, width, tiles), second_rows(tile, width, tiles), by_rows(tile, 2),
            whole(w_in.shape), whole(w_out.shape),
        ],
        [
            by_rows(tile, 2 * hidden_width), by_columns(hidden_width, tile),
            first_rows(tile, width, tiles), second_rows(tile, width, tiles),
        ],
        [
            jax.ShapeDtypeStruct((count, 2 * hidden_width), F32),
            jax.ShapeDtypeStruct((hidden_width, count), BF),
            jax.ShapeDtypeStruct((half, width), BF),
            jax.ShapeDtypeStruct((half, width), BF),
        ],
    )(first, second, gate, w_in, w_out)


def backward(first, second, act, gate, w_in, w_out, units):
    half, width = first.shape
    count = 2 * half
    hidden_width = w_out.shape[1]
    tile = tile_of(half)
    tiles = half // tile

    def body(a_ref, b_ref, act_ref, g_ref, wi_ref, wo_ref, pre_ref, out_a_ref, out_b_ref, dots_ref):
        def run(c_ref, out_ref):
            raw = jnp.dot(c_ref[...], wo_ref[...], preferred_element_type=F32)
            gate_act, up_act = act_ref[:, :hidden_width], act_ref[:, hidden_width:]
            sigma = jax.nn.sigmoid(gate_act)
            silu = gate_act * sigma
            product = silu * up_act * raw
            lane = lax.broadcasted_iota(jnp.int32, product.shape, 1)
            own = jnp.sum(jnp.where(lane < units, product, 0.0), axis=1, keepdims=True)
            hot = jnp.sum(jnp.where(lane < units, 0.0, product), axis=1, keepdims=True)
            lane = lax.broadcasted_iota(jnp.int32, dots_ref.shape, 1)
            dots_ref[...] = jnp.where(lane == 0, own, hot)
            grad = raw * row_weights(g_ref, units, raw.shape)
            gate_pre = (grad * up_act * sigma * (1.0 + gate_act * (1.0 - sigma))).astype(BF)
            up_pre = (grad * silu).astype(BF)
            pre_ref[:hidden_width, :] = gate_pre.T
            pre_ref[hidden_width:, :] = up_pre.T
            pre = jnp.concatenate([gate_pre, up_pre], axis=1)
            out_ref[...] = lax.dot_general(
                pre, wi_ref[...], OVER_COLS, preferred_element_type=F32
            ).astype(BF)

        on_both(tiles, run, (a_ref, out_a_ref), (b_ref, out_b_ref))

    return call(
        body,
        (2 * tiles,),
        [
            first_rows(tile, width, tiles), second_rows(tile, width, tiles),
            by_rows(tile, 2 * hidden_width), by_rows(tile, 2), whole(w_in.shape), whole(w_out.shape),
        ],
        [
            by_columns(2 * hidden_width, tile), first_rows(tile, width, tiles),
            second_rows(tile, width, tiles), by_rows(tile, 2),
        ],
        [
            jax.ShapeDtypeStruct((2 * hidden_width, count), BF),
            jax.ShapeDtypeStruct((half, width), BF),
            jax.ShapeDtypeStruct((half, width), BF),
            jax.ShapeDtypeStruct((count, 2), F32),
        ],
    )(first, second, act, gate, w_in, w_out)


def weight_sums(pre, xs, hidden, cs):
    half, width = xs[0].shape
    tile = min(width, 512)

    def body(pre_ref, xa_ref, xb_ref, hidden_ref, ca_ref, cb_ref, in_ref, down_ref):
        in_ref[...] = both(pre_ref, xa_ref, xb_ref)
        down_ref[...] = both(hidden_ref, ca_ref, cb_ref)

    cut = by_columns(half, tile)
    return call(
        body,
        (width // tile,),
        [whole(pre.shape), cut, cut, whole(hidden.shape), cut, cut],
        [by_columns(pre.shape[0], tile), by_columns(hidden.shape[0], tile)],
        [
            jax.ShapeDtypeStruct((pre.shape[0], width), F32),
            jax.ShapeDtypeStruct((hidden.shape[0], width), F32),
        ],
    )(pre, *xs, hidden, *cs)


def both(left_ref, a_ref, b_ref):
    half = a_ref.shape[0]
    value = jnp.dot(left_ref[:, :half], a_ref[...], preferred_element_type=F32)
    return value + jnp.dot(left_ref[:, half:], b_ref[...], preferred_element_type=F32)


def weight_totals(pre, xs, hidden, cs, in_sum, down_sum, units):
    half, width = xs[0].shape
    tile = min(width, 512)
    padded = hidden.shape[0]
    spare = padded - units

    def body(pre_ref, xa_ref, xb_ref, hidden_ref, ca_ref, cb_ref, in_ref, down_ref, own_ref, hot_ref):
        total = in_ref[...] + both(pre_ref, xa_ref, xb_ref)
        own_ref[:units, :] = total[:units].astype(BF)
        own_ref[units : 2 * units, :] = total[padded : padded + units].astype(BF)
        hot_ref[:spare, :] = total[units:padded].astype(BF)
        hot_ref[spare : 2 * spare, :] = total[padded + units :].astype(BF)
        total = down_ref[...] + both(hidden_ref, ca_ref, cb_ref)
        own_ref[2 * units :, :] = total[:units].astype(BF)
        hot_ref[2 * spare :, :] = total[units:].astype(BF)

    cut = by_columns(half, tile)
    return call(
        body,
        (width // tile,),
        [
            whole(pre.shape), cut, cut, whole(hidden.shape), cut, cut,
            by_columns(2 * padded, tile), by_columns(padded, tile),
        ],
        [by_columns(3 * units, tile), by_columns(3 * spare, tile)],
        [
            jax.ShapeDtypeStruct((3 * units, width), BF),
            jax.ShapeDtypeStruct((3 * spare, width), BF),
        ],
    )(pre, *xs, hidden, *cs, in_sum, down_sum)


def sum_of(*arrays):
    rows, width = arrays[0].shape
    tile = min(rows, 128)

    def body(*refs):
        total = refs[0][...].astype(F32)
        for ref in refs[1:-1]:
            total = total + ref[...].astype(F32)
        refs[-1][...] = total.astype(BF)

    return call(
        body,
        (rows // tile,),
        [by_rows(tile, width)] * len(arrays),
        by_rows(tile, width),
        jax.ShapeDtypeStruct((rows, width), BF),
    )(*arrays)


def halves_of_sum(*arrays):
    half, width = arrays[0].shape[0] // 2, arrays[0].shape[1]
    tile = min(half, 128)
    tiles = half // tile

    def body(*refs):
        def run(out_ref):
            total = refs[0][...].astype(F32)
            for ref in refs[1:-2]:
                total = total + ref[...].astype(F32)
            out_ref[...] = total.astype(BF)

        on_both(tiles, run, (refs[-2],), (refs[-1],))

    shape = jax.ShapeDtypeStruct((half, width), BF)
    return call(
        body,
        (2 * tiles,),
        [by_rows(tile, width)] * len(arrays),
        [first_rows(tile, width, tiles), second_rows(tile, width, tiles)],
        [shape, shape],
    )(*arrays)


def fold(*arrays):
    for step in range(len(chip_bits()) - 2, -1, -1):
        mine, other = halves_of_sum(*arrays)
        arrays = (mine, hop(other, step))
    return sum_of(*arrays)


def finish(mine, right, left, hot, is_owner):
    units, width = hot.shape[1:]

    def body(flag_ref, mine_ref, right_ref, left_ref, hot_ref, out_ref):
        total = mine_ref[...].astype(F32) + right_ref[...].astype(F32) + left_ref[...].astype(F32)
        total = jnp.where(flag_ref[0] > 0, hot_ref[0].astype(F32), total)
        out_ref[0] = total.T

    block = pl.BlockSpec((units, width), lambda i: (i, 0))
    return pl.pallas_call(
        body,
        grid=(3,),
        in_specs=[
            pl.BlockSpec(memory_space=pltpu.SMEM), block, block, block,
            pl.BlockSpec((1, units, width), lambda i: (i, 0, 0)),
        ],
        out_specs=pl.BlockSpec((1, width, units), lambda i: (i, 0, 0)),
        out_shape=jax.ShapeDtypeStruct((3, width, units), F32),
        compiler_params=pltpu.CompilerParams(vmem_limit_bytes=32 * 1024 * 1024),
    )(is_owner.astype(jnp.int32).reshape(1), mine, right, left, hot)


def hot_pieces(weights, is_owner):
    experts, groups = lax.axis_size("expert"), lax.axis_size("dp")
    width, units = weights[0].shape
    part = width // groups
    start = lax.axis_index("dp") * part
    pieces = [
        lax.dynamic_slice_in_dim(w, start, part, 0).T.reshape(experts, units // experts, part)
        for w in weights
    ]
    pieces = jnp.concatenate(pieces, axis=1)
    return jnp.where(is_owner, pieces, jnp.zeros_like(pieces))


def per_device(tokens, expert_ids, gates, w_gate, w_up, w_down, cotangent):
    experts, groups = lax.axis_size("expert"), lax.axis_size("dp")
    me, group = lax.axis_index("expert"), lax.axis_index("dp")
    tok_rows, width = tokens.shape
    units = w_gate.shape[2]
    share = units // experts
    last = len(chip_bits()) - 1
    expert_range = jnp.arange(experts, dtype=jnp.int32)
    matches = expert_ids[:, :, None] == expert_range
    hot_expert = jnp.argmax(jnp.sum(matches.astype(jnp.int32), axis=(0, 1))).astype(jnp.int32)
    is_owner = me == hot_expert
    is_me = ((expert_range == me) & ~is_owner)[:, None]
    is_hot = (expert_range == hot_expert)[:, None]
    routed = jnp.sum(jnp.where(matches, gates[:, :, None], 0.0), axis=1).T
    own = (w_gate[0], w_up[0], w_down[0])
    orders = row_order()
    x_held, c_held, r_held = tokens, cotangent, routed
    for step in range(last):
        x_held = join(x_held, hop(x_held, step))
        c_held = join(c_held, hop(c_held, step))
        r_held = jnp.concatenate([r_held, hop(r_held, step)], axis=1)
    r_last = hop(r_held, last)
    hot = hot_pieces(own, is_owner)
    bit = 1
    while bit < experts:
        hot = hot.reshape((hot.shape[0] // 2, 2) + hot.shape[1:])
        mark = (me // bit) % 2
        other = lax.dynamic_index_in_dim(hot, 1 - mark, 1, keepdims=False)
        hot = lax.dynamic_index_in_dim(hot, mark, 1, keepdims=False)
        hot = hot + flip(other, bit, bit)
        bit *= 2
    hot = hot[0]
    x_held, c_held, r_held, r_last, hot = ends_round(x_held, c_held, r_held, r_last, hot)

    x_last, c_last = hop(x_held, last), hop(c_held, last)
    x_other, c_other = swap_core(x_held), swap_core(c_held)
    r_held = jnp.concatenate([r_held, r_last], axis=1)
    r_other = swap_core(r_held)
    half = x_held.shape[0]
    own_gate, hot_gate = (
        [jnp.sum(jnp.where(mask, table, 0.0), axis=0) for table in (r_held, r_other)]
        for mask in (is_me, is_hot)
    )

    def gates_of(part):
        columns = [
            jnp.concatenate([value[part] for value in values]) for values in (own_gate, hot_gate)
        ]
        return jnp.stack(columns).T

    gate_near, gate_far = gates_of(slice(None, half)), gates_of(slice(half, None))
    spare = share + -(units + share) % 128
    hot = line_gather(hot).reshape(3, share, width)
    hot = jnp.pad(hot, ((0, 0), (0, spare - share), (0, 0))).reshape(3 * spare, width).T
    w_in = jnp.concatenate([own[0], hot[:, :spare], own[1], hot[:, spare : 2 * spare]], axis=1)
    w_out = jnp.concatenate([own[2], hot[:, 2 * spare :]], axis=1)
    a_near, s_near, m_near, m_near_far = forward(x_held, x_other, gate_near, w_in, w_out, units)
    p_near, t_near, t_near_far, d_near = backward(
        c_held, c_other, a_near, gate_near, w_in, w_out, units
    )
    (
        x_last, c_last, m_near, m_near_far, t_near, t_near_far, d_near, gate_far,
        w_in, w_out, p_near, s_near, x_held, x_other, c_held, c_other,
    ) = ends_round(
        x_last, c_last, m_near, m_near_far, t_near, t_near_far, d_near, gate_far,
        w_in, w_out, p_near, s_near, x_held, x_other, c_held, c_other,
    )

    x_last_other, c_last_other = swap_core(x_last), swap_core(c_last)
    in_near, down_near = weight_sums(p_near, (x_held, x_other), s_near, (c_held, c_other))
    x_last, x_last_other, c_last, c_last_other, m_near, m_near_far, t_near, t_near_far, in_near, down_near = (
        ends_round(
            x_last, x_last_other, c_last, c_last_other, m_near, m_near_far, t_near, t_near_far,
            in_near, down_near,
        )
    )

    m_near_other, t_near_other = swap_core(m_near_far), swap_core(t_near_far)
    a_far, s_far, m_far, m_far_far = forward(x_last, x_last_other, gate_far, w_in, w_out, units)
    m_far_other = swap_core(m_far_far)
    p_far, t_far, t_far_far, d_far = backward(
        c_last, c_last_other, a_far, gate_far, w_in, w_out, units
    )
    own_grad, hot_grad = weight_totals(
        p_far, (x_last, x_last_other), s_far, (c_last, c_last_other), in_near, down_near, units
    )
    line = LineSum(own_grad)
    right, left = line.sends(1)
    right, left, m_far, m_far_other, t_far, t_far_far, d_far, hot_grad, m_near, m_near_other = ends_round(
        right, left, m_far, m_far_other, t_far, t_far_far, d_far, hot_grad, m_near, m_near_other
    )

    line.send(1, right, left)
    m_got = hop(sum_of(m_far, m_far_other), last)
    t_far_other = swap_core(t_far_far)
    hot_grad = hot_grad.reshape(3, spare, width)[:, :share].reshape(3 * share, width)
    hot_sum = lax.psum_scatter(hot_grad, "dp", scatter_dimension=1, tiled=True)
    t_far, t_far_other, m_got, line.right, line.left = ends_round(
        t_far, t_far_other, m_got, line.right, line.left
    )

    right, left = line.sends(2)
    right, left, t_far, t_far_other, m_got, m_near, m_near_other = ends_round(
        right, left, t_far, t_far_other, m_got, m_near, m_near_other
    )
    line.send(2, right, left)
    t_got = hop(sum_of(t_far, t_far_other), last)
    mixed = fold(m_near, m_near_other, m_got)
    dots = lax.all_gather(jnp.concatenate([d_near, d_far]).T, "expert", axis=0)
    mixed, t_got, dots, hot_sum, line.right, line.left = ends_round(
        mixed, t_got, dots, hot_sum, line.right, line.left
    )

    for step in range(3, groups):
        right, left = line.sends(step)
        right, left, t_near, t_near_other, t_got = ends_round(right, left, t_near, t_near_other, t_got)
        line.send(step, right, left)
    tokens_grad = fold(t_near, t_near_other, t_got)
    hot_all = lax.all_gather(hot_sum.astype(BF), "expert", axis=0)

    my_dots = []
    for source in range(experts):
        order = orders[source % 2]
        place = jnp.array([order.index(r) for r in range(experts)], jnp.int32)
        place = jnp.sum(jnp.where(expert_range == (me ^ source), place, 0))
        my_dots.append(lax.dynamic_slice_in_dim(dots[source], place * tok_rows, tok_rows, 1))
    my_dots = jnp.stack(my_dots)
    hot_dot = jnp.sum(my_dots[:, 1], axis=0)
    own_dot = jnp.sum(jnp.where(matches, my_dots[:, 0].T[:, None, :], 0.0), axis=2)
    gates_grad = jnp.where(expert_ids == hot_expert, hot_dot[:, None], own_dot)

    hot_all = hot_all.reshape(experts, 3, share, width // groups)
    hot_all = jnp.moveaxis(hot_all, 1, 0).reshape(3, units, width // groups)
    grads = finish(line.block(group), line.right, line.left, hot_all, is_owner)
    return (mixed, tokens_grad, gates_grad, grads[0:1], grads[1:2], grads[2:3])


def solution(mesh):
    rows = P(("dp", "expert"), None)
    weight = P("expert", None, None)
    grad = P("expert", "dp", None)
    return jax.shard_map(
        per_device,
        mesh=mesh,
        in_specs=(rows, rows, rows, weight, weight, weight, rows),
        out_specs=(rows, rows, rows, grad, grad, grad),
        check_vma=False,
    )
```

```python
import jax
import jax.numpy as jnp
from jax import lax
from jax.experimental import pallas as pl
from jax.experimental.pallas import tpu as pltpu
from jax.sharding import PartitionSpec as P

BF = jnp.bfloat16
F32 = jnp.float32
OVER_ROWS = (((0,), (0,)), ((), ()))
OVER_COLS = (((1,), (1,)), ((), ()))


def add(left, right):
    return (left.astype(F32) + right.astype(F32)).astype(BF)


def join(*values):
    return jnp.concatenate(values, axis=0)


def ends_round(*values):
    return lax.optimization_barrier(values)


def chip_bits():
    return [1 << b for b in range(1, lax.axis_size("expert").bit_length() - 1)]


def flip(value, bit_even, bit_odd):
    size = lax.axis_size("expert")
    pairs = [(i, i ^ (bit_odd if i & 1 else bit_even)) for i in range(size)]
    return lax.ppermute(value, "expert", pairs)


def swap_core(value):
    return flip(value, 1, 1)


def hop(value, step):
    bits = chip_bits()
    return flip(value, bits[step], bits[-1 - step])


def take(stacked, index):
    return lax.dynamic_index_in_dim(stacked, index, 0, keepdims=False)


class LineSum:
    def __init__(self, part):
        self.part = part
        self.size = lax.axis_size("dp")
        self.right, self.left = None, None

    def block(self, index):
        width = self.part.shape[1] // self.size
        start = jnp.clip(index, 0, self.size - 1) * width
        return lax.dynamic_slice_in_dim(self.part, start, width, 1)

    def sends(self, step):
        size, me = self.size, lax.axis_index("dp")
        right, left = self.block(size - step + me), self.block(me - (size - step))
        if step > 1:
            right, left = add(right, self.right), add(left, self.left)
        return right, left

    def send(self, step, right, left):
        size = self.size
        self.right = lax.ppermute(right, "dp", [(i, i + 1) for i in range(step)])
        self.left = lax.ppermute(left, "dp", [(size - 1 - i, size - 2 - i) for i in range(step)])

def line_gather(mine):
    groups = lax.axis_size("dp")
    group = lax.axis_index("dp")
    found = mine[None]
    bit = 1
    while bit < groups:
        found = join(found, lax.ppermute(found, "dp", [(i, i ^ bit) for i in range(groups)]))
        bit *= 2
    return jnp.concatenate([take(found, group ^ j) for j in range(groups)], axis=1)


def row_order():
    lists = []
    for bits in (chip_bits(), chip_bits()[::-1]):
        held = [0]
        for bit in bits:
            held = held + [r ^ bit for r in held]
        lists.append(held)
    half = len(lists[0]) // 2
    orders = []
    for core in (0, 1):
        own, other = lists[core], [r ^ 1 for r in lists[1 - core]]
        orders.append(own[:half] + other[:half] + own[half:] + other[half:])
    return orders


def tile_of(rows):
    tile = min(rows, 256)
    assert rows % tile == 0
    return tile


def call(body, grid, in_specs, out_specs, out_shape):
    return pl.pallas_call(
        body,
        grid=grid,
        in_specs=in_specs,
        out_specs=out_specs,
        out_shape=out_shape,
        cost_estimate=pl.CostEstimate(flops=1000, bytes_accessed=1000, transcendentals=0),
        compiler_params=pltpu.CompilerParams(
            dimension_semantics=("arbitrary",), vmem_limit_bytes=60 * 1024 * 1024
        ),
    )


def by_rows(tile, width):
    return pl.BlockSpec((tile, width), lambda i: (i, 0))


def by_columns(height, tile):
    return pl.BlockSpec((height, tile), lambda i: (0, i))


def whole(shape):
    return pl.BlockSpec(shape, lambda i: (0, 0))


def row_weights(gate_ref, units, shape):
    lane = lax.broadcasted_iota(jnp.int32, shape, 1)
    return jnp.where(lane < units, gate_ref[:, 0:1], gate_ref[:, 1:2])


def first_rows(tile, width, tiles):
    return pl.BlockSpec((tile, width), lambda i: (jnp.minimum(i, tiles - 1), 0))


def second_rows(tile, width, tiles):
    return pl.BlockSpec((tile, width), lambda i: (jnp.maximum(i - tiles, 0), 0))


def on_both(tiles, run, first, second):
    pl.when(pl.program_id(0) < tiles)(lambda: run(*first))
    pl.when(pl.program_id(0) >= tiles)(lambda: run(*second))


def forward(first, second, gate, w_in, w_out, units):
    half, width = first.shape
    count = 2 * half
    hidden_width = w_out.shape[1]
    tile = tile_of(half)
    tiles = half // tile

    def body(a_ref, b_ref, g_ref, wi_ref, wo_ref, act_ref, hidden_ref, out_a_ref, out_b_ref):
        def run(x_ref, out_ref):
            act = jnp.dot(x_ref[...], wi_ref[...], preferred_element_type=F32)
            act_ref[...] = act
            gate_act, up_act = act[:, :hidden_width], act[:, hidden_width:]
            weight = row_weights(g_ref, units, gate_act.shape)
            hidden = (gate_act * jax.nn.sigmoid(gate_act) * up_act * weight).astype(BF)
            hidden_ref[...] = hidden.T
            out_ref[...] = lax.dot_general(
                hidden, wo_ref[...], OVER_COLS, preferred_element_type=F32
            ).astype(BF)

        on_both(tiles, run, (a_ref, out_a_ref), (b_ref, out_b_ref))

    return call(
        body,
        (2 * tiles,),
        [
            first_rows(tile, width, tiles), second_rows(tile, width, tiles), by_rows(tile, 2),
            whole(w_in.shape), whole(w_out.shape),
        ],
        [
            by_rows(tile, 2 * hidden_width), by_columns(hidden_width, tile),
            first_rows(tile, width, tiles), second_rows(tile, width, tiles),
        ],
        [
            jax.ShapeDtypeStruct((count, 2 * hidden_width), F32),
            jax.ShapeDtypeStruct((hidden_width, count), BF),
            jax.ShapeDtypeStruct((half, width), BF),
            jax.ShapeDtypeStruct((half, width), BF),
        ],
    )(first, second, gate, w_in, w_out)


def backward(first, second, act, gate, w_in, w_out, units):
    half, width = first.shape
    count = 2 * half
    hidden_width = w_out.shape[1]
    tile = tile_of(half)
    tiles = half // tile

    def body(a_ref, b_ref, act_ref, g_ref, wi_ref, wo_ref, pre_ref, out_a_ref, out_b_ref, dots_ref):
        def run(c_ref, out_ref):
            raw = jnp.dot(c_ref[...], wo_ref[...], preferred_element_type=F32)
            gate_act, up_act = act_ref[:, :hidden_width], act_ref[:, hidden_width:]
            sigma = jax.nn.sigmoid(gate_act)
            silu = gate_act * sigma
            product = silu * up_act * raw
            lane = lax.broadcasted_iota(jnp.int32, product.shape, 1)
            own = jnp.sum(jnp.where(lane < units, product, 0.0), axis=1, keepdims=True)
            hot = jnp.sum(jnp.where(lane < units, 0.0, product), axis=1, keepdims=True)
            lane = lax.broadcasted_iota(jnp.int32, dots_ref.shape, 1)
            dots_ref[...] = jnp.where(lane == 0, own, hot)
            grad = raw * row_weights(g_ref, units, raw.shape)
            gate_pre = (grad * up_act * sigma * (1.0 + gate_act * (1.0 - sigma))).astype(BF)
            up_pre = (grad * silu).astype(BF)
            pre_ref[:hidden_width, :] = gate_pre.T
            pre_ref[hidden_width:, :] = up_pre.T
            pre = jnp.concatenate([gate_pre, up_pre], axis=1)
            out_ref[...] = lax.dot_general(
                pre, wi_ref[...], OVER_COLS, preferred_element_type=F32
            ).astype(BF)

        on_both(tiles, run, (a_ref, out_a_ref), (b_ref, out_b_ref))

    return call(
        body,
        (2 * tiles,),
        [
            first_rows(tile, width, tiles), second_rows(tile, width, tiles),
            by_rows(tile, 2 * hidden_width), by_rows(tile, 2), whole(w_in.shape), whole(w_out.shape),
        ],
        [
            by_columns(2 * hidden_width, tile), first_rows(tile, width, tiles),
            second_rows(tile, width, tiles), by_rows(tile, 2),
        ],
        [
            jax.ShapeDtypeStruct((2 * hidden_width, count), BF),
            jax.ShapeDtypeStruct((half, width), BF),
            jax.ShapeDtypeStruct((half, width), BF),
            jax.ShapeDtypeStruct((count, 2), F32),
        ],
    )(first, second, act, gate, w_in, w_out)


def weight_sums(pre, xs, hidden, cs):
    half, width = xs[0].shape
    tile = min(width, 512)

    def body(pre_ref, xa_ref, xb_ref, hidden_ref, ca_ref, cb_ref, in_ref, down_ref):
        in_ref[...] = both(pre_ref, xa_ref, xb_ref)
        down_ref[...] = both(hidden_ref, ca_ref, cb_ref)

    cut = by_columns(half, tile)
    return call(
        body,
        (width // tile,),
        [whole(pre.shape), cut, cut, whole(hidden.shape), cut, cut],
        [by_columns(pre.shape[0], tile), by_columns(hidden.shape[0], tile)],
        [
            jax.ShapeDtypeStruct((pre.shape[0], width), F32),
            jax.ShapeDtypeStruct((hidden.shape[0], width), F32),
        ],
    )(pre, *xs, hidden, *cs)


def both(left_ref, a_ref, b_ref):
    half = a_ref.shape[0]
    value = jnp.dot(left_ref[:, :half], a_ref[...], preferred_element_type=F32)
    return value + jnp.dot(left_ref[:, half:], b_ref[...], preferred_element_type=F32)


def weight_totals(pre, xs, hidden, cs, in_sum, down_sum, units):
    half, width = xs[0].shape
    tile = min(width, 512)
    padded = hidden.shape[0]
    spare = padded - units

    def body(pre_ref, xa_ref, xb_ref, hidden_ref, ca_ref, cb_ref, in_ref, down_ref, own_ref, hot_ref):
        total = in_ref[...] + both(pre_ref, xa_ref, xb_ref)
        own_ref[:units, :] = total[:units].astype(BF)
        own_ref[units : 2 * units, :] = total[padded : padded + units].astype(BF)
        hot_ref[:spare, :] = total[units:padded].astype(BF)
        hot_ref[spare : 2 * spare, :] = total[padded + units :].astype(BF)
        total = down_ref[...] + both(hidden_ref, ca_ref, cb_ref)
        own_ref[2 * units :, :] = total[:units].astype(BF)
        hot_ref[2 * spare :, :] = total[units:].astype(BF)

    cut = by_columns(half, tile)
    return call(
        body,
        (width // tile,),
        [
            whole(pre.shape), cut, cut, whole(hidden.shape), cut, cut,
            by_columns(2 * padded, tile), by_columns(padded, tile),
        ],
        [by_columns(3 * units, tile), by_columns(3 * spare, tile)],
        [
            jax.ShapeDtypeStruct((3 * units, width), BF),
            jax.ShapeDtypeStruct((3 * spare, width), BF),
        ],
    )(pre, *xs, hidden, *cs, in_sum, down_sum)


def sum_of(*arrays):
    rows, width = arrays[0].shape
    tile = min(rows, 128)

    def body(*refs):
        total = refs[0][...].astype(F32)
        for ref in refs[1:-1]:
            total = total + ref[...].astype(F32)
        refs[-1][...] = total.astype(BF)

    return call(
        body,
        (rows // tile,),
        [by_rows(tile, width)] * len(arrays),
        by_rows(tile, width),
        jax.ShapeDtypeStruct((rows, width), BF),
    )(*arrays)


def halves_of_sum(*arrays, split=()):
    half, width = arrays[0].shape[0] // 2, arrays[0].shape[1]
    tile = min(half, 128)
    tiles = half // tile
    count = len(arrays)

    def body(*refs):
        def run(out_ref, more):
            total = refs[0][...].astype(F32)
            for ref in refs[1:count] + more:
                total = total + ref[...].astype(F32)
            out_ref[...] = total.astype(BF)

        more = refs[count:-2]
        on_both(tiles, run, (refs[-2], more[:1]), (refs[-1], more[1:]))

    shape = jax.ShapeDtypeStruct((half, width), BF)
    ends = [first_rows(tile, width, tiles), second_rows(tile, width, tiles)]
    return call(
        body,
        (2 * tiles,),
        [by_rows(tile, width)] * count + ends[: len(split)],
        ends,
        [shape, shape],
    )(*arrays, *split)


def last_hop(mine, other):
    step = len(chip_bits()) - 1
    return [hop(part, step) for part in halves_of_sum(mine, other)]


def fold(mine, got):
    arrays, split = ((mine,), tuple(got)) if isinstance(got, list) else ((mine, got), ())
    for step in range(len(chip_bits()) - 2, -1, -1):
        mine, other = halves_of_sum(*arrays, split=split)
        arrays, split = (mine, hop(other, step)), ()
    return sum_of(*arrays)


def finish(mine, right, left, hot, is_owner):
    units, width = hot.shape[1:]

    def body(flag_ref, mine_ref, right_ref, left_ref, hot_ref, *out_refs):
        for index, out_ref in enumerate(out_refs):
            rows = slice(index * units, (index + 1) * units)
            total = mine_ref[rows].astype(F32) + right_ref[rows].astype(F32) + left_ref[rows].astype(F32)
            total = jnp.where(flag_ref[0] > 0, hot_ref[index].astype(F32), total)
            out_ref[0] = total.T

    block = whole((3 * units, width))
    return pl.pallas_call(
        body,
        grid=(1,),
        in_specs=[
            pl.BlockSpec(memory_space=pltpu.SMEM), block, block, block,
            pl.BlockSpec((3, units, width), lambda i: (0, 0, 0)),
        ],
        out_specs=[pl.BlockSpec((1, width, units), lambda i: (0, 0, 0))] * 3,
        out_shape=[jax.ShapeDtypeStruct((1, width, units), F32)] * 3,
        compiler_params=pltpu.CompilerParams(vmem_limit_bytes=60 * 1024 * 1024),
    )(is_owner.astype(jnp.int32).reshape(1), mine, right, left, hot)


def hot_pieces(weights, is_owner):
    width, units = weights[0].shape
    part = width // lax.axis_size("dp")
    scalars = jnp.stack([lax.axis_index("dp"), is_owner.astype(jnp.int32)]).astype(jnp.int32)

    def body(scalar_ref, a_ref, b_ref, c_ref, out_ref):
        for index, ref in enumerate((a_ref, b_ref, c_ref)):
            out_ref[index] = ref[...].T

        @pl.when(scalar_ref[1] == 0)
        def _():
            out_ref[...] = jnp.zeros_like(out_ref)

    return pl.pallas_call(
        body,
        grid_spec=pltpu.PrefetchScalarGridSpec(
            num_scalar_prefetch=1,
            grid=(1,),
            in_specs=[pl.BlockSpec((part, units), lambda i, scalars: (scalars[0], 0))] * 3,
            out_specs=pl.BlockSpec((3, units, part), lambda i, scalars: (0, 0, 0)),
        ),
        out_shape=jax.ShapeDtypeStruct((3, units, part), BF),
        cost_estimate=pl.CostEstimate(flops=1000, bytes_accessed=1000, transcendentals=0),
        compiler_params=pltpu.CompilerParams(vmem_limit_bytes=60 * 1024 * 1024),
    )(scalars, *weights)


def widen(weights, hot):
    width, units = weights[0].shape
    spare = hot.shape[1]
    tile = tile_of(width)

    def body(gate_ref, up_ref, down_ref, hot_ref, in_ref, out_ref):
        padded = units + spare
        in_ref[:, :units] = gate_ref[...]
        in_ref[:, units:padded] = hot_ref[0].T
        in_ref[:, padded : padded + units] = up_ref[...]
        in_ref[:, padded + units :] = hot_ref[1].T
        out_ref[:, :units] = down_ref[...]
        out_ref[:, units:] = hot_ref[2].T

    rows = by_rows(tile, units)
    return call(
        body,
        (width // tile,),
        [rows, rows, rows, pl.BlockSpec((3, spare, tile), lambda i: (0, 0, i))],
        [by_rows(tile, 2 * (units + spare)), by_rows(tile, units + spare)],
        [
            jax.ShapeDtypeStruct((width, 2 * (units + spare)), BF),
            jax.ShapeDtypeStruct((width, units + spare), BF),
        ],
    )(*weights, hot)


def per_device(tokens, expert_ids, gates, w_gate, w_up, w_down, cotangent):
    experts, groups = lax.axis_size("expert"), lax.axis_size("dp")
    me, group = lax.axis_index("expert"), lax.axis_index("dp")
    tok_rows, width = tokens.shape
    units = w_gate.shape[2]
    share = units // experts
    last = len(chip_bits()) - 1
    expert_range = jnp.arange(experts, dtype=jnp.int32)
    matches = expert_ids[:, :, None] == expert_range
    hot_expert = jnp.argmax(jnp.sum(matches.astype(jnp.int32), axis=(0, 1))).astype(jnp.int32)
    is_owner = jnp.sum((expert_ids == me).astype(jnp.int32)) == tok_rows
    is_me = ((expert_range == me) & ~is_owner)[:, None]
    is_hot = (expert_range == hot_expert)[:, None]
    routed = jnp.sum(jnp.where(matches, gates[:, :, None], 0.0), axis=1).T
    own = (w_gate[0], w_up[0], w_down[0])
    orders = row_order()
    def halve(value, bit):
        value = value.reshape(3, value.shape[1] // 2, 2, share, width // groups)
        mark = (me // bit) % 2
        other = lax.dynamic_index_in_dim(value, 1 - mark, 2, keepdims=False)
        return lax.dynamic_index_in_dim(value, mark, 2, keepdims=False) + flip(other, bit, bit)

    x_got, c_got, r_got = hop(tokens, 0), hop(cotangent, 0), hop(routed, 0)
    hot = hot_pieces(own, is_owner).reshape(3, experts, share, width // groups)
    hot = halve(hot, 1)
    x_got, c_got, r_got, hot = ends_round(x_got, c_got, r_got, hot)

    x_held, c_held = join(tokens, x_got), join(cotangent, c_got)
    r_held = jnp.concatenate([routed, r_got], axis=1)
    for step in range(1, last):
        x_held = join(x_held, hop(x_held, step))
        c_held = join(c_held, hop(c_held, step))
        r_held = jnp.concatenate([r_held, hop(r_held, step)], axis=1)
    bit = 2
    while bit < experts:
        hot = halve(hot, bit)
        bit *= 2
    r_last = hop(r_held, last)
    x_held, c_held, r_held, r_last, hot = ends_round(x_held, c_held, r_held, r_last, hot)

    x_last, c_last = hop(x_held, last), hop(c_held, last)
    x_other, c_other = swap_core(x_held), swap_core(c_held)
    r_held = jnp.concatenate([r_held, r_last], axis=1)
    r_other = swap_core(r_held)
    half = x_held.shape[0]
    own_gate, hot_gate = (
        [jnp.sum(jnp.where(mask, table, 0.0), axis=0) for table in (r_held, r_other)]
        for mask in (is_me, is_hot)
    )

    def gates_of(part):
        columns = [
            jnp.concatenate([value[part] for value in values]) for values in (own_gate, hot_gate)
        ]
        return jnp.stack(columns).T

    gate_near, gate_far = gates_of(slice(None, half)), gates_of(slice(half, None))
    hot = line_gather(hot.reshape(3 * share, width // groups)).reshape(3, share, width)
    spare = share + -(units + share) % 128
    w_in, w_out = widen(own, jnp.pad(hot, ((0, 0), (0, spare - share), (0, 0))))
    a_near, s_near, m_near, m_near_far = forward(x_held, x_other, gate_near, w_in, w_out, units)
    p_near, t_near, t_near_far, d_near = backward(
        c_held, c_other, a_near, gate_near, w_in, w_out, units
    )
    (
        x_last, c_last, m_near, m_near_far, t_near, t_near_far, d_near, gate_far,
        w_in, w_out, p_near, s_near, x_held, x_other, c_held, c_other,
    ) = ends_round(
        x_last, c_last, m_near, m_near_far, t_near, t_near_far, d_near, gate_far,
        w_in, w_out, p_near, s_near, x_held, x_other, c_held, c_other,
    )

    x_last_other, c_last_other = swap_core(x_last), swap_core(c_last)
    in_near, down_near = weight_sums(p_near, (x_held, x_other), s_near, (c_held, c_other))
    x_last, x_last_other, c_last, c_last_other, m_near, m_near_far, t_near, t_near_far, in_near, down_near = (
        ends_round(
            x_last, x_last_other, c_last, c_last_other, m_near, m_near_far, t_near, t_near_far,
            in_near, down_near,
        )
    )

    m_near_other, t_near_other = swap_core(m_near_far), swap_core(t_near_far)
    a_far, s_far, m_far, m_far_far = forward(x_last, x_last_other, gate_far, w_in, w_out, units)
    m_far_other = swap_core(m_far_far)
    p_far, t_far, t_far_far, d_far = backward(
        c_last, c_last_other, a_far, gate_far, w_in, w_out, units
    )
    t_far_other = swap_core(t_far_far)
    own_grad, hot_grad = weight_totals(
        p_far, (x_last, x_last_other), s_far, (c_last, c_last_other), in_near, down_near, units
    )
    line = LineSum(own_grad)
    right, left = line.sends(1)
    (
        right, left, m_far, m_far_other, t_far, t_far_other, d_far, hot_grad,
        m_near, m_near_other, t_near, t_near_other,
    ) = ends_round(
        right, left, m_far, m_far_other, t_far, t_far_other, d_far, hot_grad,
        m_near, m_near_other, t_near, t_near_other,
    )

    line.send(1, right, left)
    m_got = last_hop(m_far, m_far_other)
    t_far = sum_of(t_far, t_far_other)
    m_near, t_near = sum_of(m_near, m_near_other), sum_of(t_near, t_near_other)
    hot_grad = hot_grad.reshape(3, spare, width)[:, :share].reshape(3 * share, width)
    hot_sum = lax.psum_scatter(hot_grad, "dp", scatter_dimension=1, tiled=True)
    t_far, m_near, t_near, line.right, line.left, *m_got = ends_round(
        t_far, m_near, t_near, line.right, line.left, *m_got
    )

    right, left = line.sends(2)
    right, left, t_far, m_near, *m_got = ends_round(right, left, t_far, m_near, *m_got)
    line.send(2, right, left)
    t_got = hop(t_far, last)
    mixed = fold(m_near, m_got)
    dots = lax.all_gather(jnp.concatenate([d_near, d_far]).T, "expert", axis=0)
    mixed, t_got, dots, hot_sum, line.right, line.left = ends_round(
        mixed, t_got, dots, hot_sum, line.right, line.left
    )

    for step in range(3, groups):
        right, left = line.sends(step)
        right, left, t_near, t_got = ends_round(right, left, t_near, t_got)
        line.send(step, right, left)
    tokens_grad = fold(t_near, t_got)
    hot_all = lax.all_gather(hot_sum.astype(BF), "expert", axis=0)

    my_dots = []
    for source in range(experts):
        order = orders[source % 2]
        place = jnp.array([order.index(r) for r in range(experts)], jnp.int32)
        place = jnp.sum(jnp.where(expert_range == (me ^ source), place, 0))
        my_dots.append(lax.dynamic_slice_in_dim(dots[source], place * tok_rows, tok_rows, 1))
    my_dots = jnp.stack(my_dots)
    hot_dot = jnp.sum(my_dots[:, 1], axis=0)
    own_dot = jnp.sum(jnp.where(matches, my_dots[:, 0].T[:, None, :], 0.0), axis=2)
    gates_grad = jnp.where(expert_ids == hot_expert, hot_dot[:, None], own_dot)

    hot_all = hot_all.reshape(experts, 3, share, width // groups)
    hot_all = jnp.moveaxis(hot_all, 1, 0).reshape(3, units, width // groups)
    grads = finish(line.block(group), line.right, line.left, hot_all, is_owner)
    return (mixed, tokens_grad, gates_grad, *grads)


def solution(mesh):
    rows = P(("dp", "expert"), None)
    weight = P("expert", None, None)
    grad = P("expert", "dp", None)
    return jax.shard_map(
        per_device,
        mesh=mesh,
        in_specs=(rows, rows, rows, weight, weight, weight, rows),
        out_specs=(rows, rows, rows, grad, grad, grad),
        check_vma=False,
    )
```

```python
import jax
import jax.numpy as jnp
from jax import lax
from jax.experimental import pallas as pl
from jax.experimental.pallas import tpu as pltpu
from jax.sharding import PartitionSpec as P

BF = jnp.bfloat16
F32 = jnp.float32
OVER_ROWS = (((0,), (0,)), ((), ()))
OVER_COLS = (((1,), (1,)), ((), ()))


def add(left, right):
    return (left.astype(F32) + right.astype(F32)).astype(BF)


def join(*values):
    return jnp.concatenate(values, axis=0)


def ends_round(*values):
    return lax.optimization_barrier(values)


def chip_bits():
    return [1 << b for b in range(1, lax.axis_size("expert").bit_length() - 1)]


def flip(value, bit_even, bit_odd):
    size = lax.axis_size("expert")
    pairs = [(i, i ^ (bit_odd if i & 1 else bit_even)) for i in range(size)]
    return lax.ppermute(value, "expert", pairs)


def swap_core(value):
    return flip(value, 1, 1)


def hop(value, step):
    bits = chip_bits()
    return flip(value, bits[step], bits[-1 - step])


def take(stacked, index):
    return lax.dynamic_index_in_dim(stacked, index, 0, keepdims=False)


class LineSum:
    def __init__(self, part):
        self.part = part
        self.size = lax.axis_size("dp")
        self.right, self.left = None, None

    def block(self, index):
        width = self.part.shape[1] // self.size
        start = jnp.clip(index, 0, self.size - 1) * width
        return lax.dynamic_slice_in_dim(self.part, start, width, 1)

    def sends(self, step):
        size, me = self.size, lax.axis_index("dp")
        right, left = self.block(size - step + me), self.block(me - (size - step))
        if step > 1:
            right, left = add(right, self.right), add(left, self.left)
        return right, left

    def send(self, step, right, left):
        size = self.size
        self.right = lax.ppermute(right, "dp", [(i, i + 1) for i in range(step)])
        self.left = lax.ppermute(left, "dp", [(size - 1 - i, size - 2 - i) for i in range(step)])

def line_gather(mine):
    groups = lax.axis_size("dp")
    group = lax.axis_index("dp")
    found = mine[None]
    bit = 1
    while bit < groups:
        found = join(found, lax.ppermute(found, "dp", [(i, i ^ bit) for i in range(groups)]))
        bit *= 2
    return jnp.concatenate([take(found, group ^ j) for j in range(groups)], axis=1)


def row_order():
    lists = []
    for bits in (chip_bits(), chip_bits()[::-1]):
        held = [0]
        for bit in bits:
            held = held + [r ^ bit for r in held]
        lists.append(held)
    half = len(lists[0]) // 2
    orders = []
    for core in (0, 1):
        own, other = lists[core], [r ^ 1 for r in lists[1 - core]]
        orders.append(own[:half] + other[:half] + own[half:] + other[half:])
    return orders


def tile_of(rows):
    tile = min(rows, 512)
    assert rows % tile == 0
    return tile


def call(body, grid, in_specs, out_specs, out_shape):
    return pl.pallas_call(
        body,
        grid=grid,
        in_specs=in_specs,
        out_specs=out_specs,
        out_shape=out_shape,
        cost_estimate=pl.CostEstimate(flops=1000, bytes_accessed=1000, transcendentals=0),
        compiler_params=pltpu.CompilerParams(
            dimension_semantics=("arbitrary",), vmem_limit_bytes=60 * 1024 * 1024
        ),
    )


def by_rows(tile, width):
    return pl.BlockSpec((tile, width), lambda i: (i, 0))


def by_columns(height, tile):
    return pl.BlockSpec((height, tile), lambda i: (0, i))


def whole(shape):
    return pl.BlockSpec(shape, lambda i: (0, 0))


def row_weights(gate_ref, units, shape):
    lane = lax.broadcasted_iota(jnp.int32, shape, 1)
    return jnp.where(lane < units, gate_ref[:, 0:1], gate_ref[:, 1:2])


def first_rows(tile, width, tiles):
    return pl.BlockSpec((tile, width), lambda i: (jnp.minimum(i, tiles - 1), 0))


def second_rows(tile, width, tiles):
    return pl.BlockSpec((tile, width), lambda i: (jnp.maximum(i - tiles, 0), 0))


def on_both(tiles, run, first, second):
    pl.when(pl.program_id(0) < tiles)(lambda: run(*first))
    pl.when(pl.program_id(0) >= tiles)(lambda: run(*second))


def forward(first, second, gate, w_in, w_out, units):
    half, width = first.shape
    count = 2 * half
    hidden_width = w_out.shape[1]
    tile = tile_of(half)
    tiles = half // tile

    def body(a_ref, b_ref, g_ref, wi_ref, wo_ref, act_ref, hidden_ref, out_a_ref, out_b_ref):
        def run(x_ref, out_ref):
            act = jnp.dot(x_ref[...], wi_ref[...], preferred_element_type=F32)
            act_ref[...] = act
            gate_act, up_act = act[:, :hidden_width], act[:, hidden_width:]
            weight = row_weights(g_ref, units, gate_act.shape)
            hidden = (gate_act * jax.nn.sigmoid(gate_act) * up_act * weight).astype(BF)
            hidden_ref[...] = hidden.T
            out_ref[...] = lax.dot_general(
                hidden, wo_ref[...], OVER_COLS, preferred_element_type=F32
            ).astype(BF)

        on_both(tiles, run, (a_ref, out_a_ref), (b_ref, out_b_ref))

    return call(
        body,
        (2 * tiles,),
        [
            first_rows(tile, width, tiles), second_rows(tile, width, tiles), by_rows(tile, 2),
            whole(w_in.shape), whole(w_out.shape),
        ],
        [
            by_rows(tile, 2 * hidden_width), by_columns(hidden_width, tile),
            first_rows(tile, width, tiles), second_rows(tile, width, tiles),
        ],
        [
            jax.ShapeDtypeStruct((count, 2 * hidden_width), F32),
            jax.ShapeDtypeStruct((hidden_width, count), BF),
            jax.ShapeDtypeStruct((half, width), BF),
            jax.ShapeDtypeStruct((half, width), BF),
        ],
    )(first, second, gate, w_in, w_out)


def backward(first, second, act, gate, w_in, w_out, units):
    half, width = first.shape
    count = 2 * half
    hidden_width = w_out.shape[1]
    tile = tile_of(half)
    tiles = half // tile

    def body(a_ref, b_ref, act_ref, g_ref, wi_ref, wo_ref, pre_ref, out_a_ref, out_b_ref, dots_ref):
        def run(c_ref, out_ref):
            raw = jnp.dot(c_ref[...], wo_ref[...], preferred_element_type=F32)
            gate_act, up_act = act_ref[:, :hidden_width], act_ref[:, hidden_width:]
            sigma = jax.nn.sigmoid(gate_act)
            silu = gate_act * sigma
            product = silu * up_act * raw
            lane = lax.broadcasted_iota(jnp.int32, product.shape, 1)
            own = jnp.sum(jnp.where(lane < units, product, 0.0), axis=1, keepdims=True)
            hot = jnp.sum(jnp.where(lane < units, 0.0, product), axis=1, keepdims=True)
            lane = lax.broadcasted_iota(jnp.int32, dots_ref.shape, 1)
            dots_ref[...] = jnp.where(lane == 0, own, hot)
            grad = raw * row_weights(g_ref, units, raw.shape)
            gate_pre = (grad * up_act * sigma * (1.0 + gate_act * (1.0 - sigma))).astype(BF)
            up_pre = (grad * silu).astype(BF)
            pre_ref[:hidden_width, :] = gate_pre.T
            pre_ref[hidden_width:, :] = up_pre.T
            pre = jnp.concatenate([gate_pre, up_pre], axis=1)
            out_ref[...] = lax.dot_general(
                pre, wi_ref[...], OVER_COLS, preferred_element_type=F32
            ).astype(BF)

        on_both(tiles, run, (a_ref, out_a_ref), (b_ref, out_b_ref))

    return call(
        body,
        (2 * tiles,),
        [
            first_rows(tile, width, tiles), second_rows(tile, width, tiles),
            by_rows(tile, 2 * hidden_width), by_rows(tile, 2), whole(w_in.shape), whole(w_out.shape),
        ],
        [
            by_columns(2 * hidden_width, tile), first_rows(tile, width, tiles),
            second_rows(tile, width, tiles), by_rows(tile, 2),
        ],
        [
            jax.ShapeDtypeStruct((2 * hidden_width, count), BF),
            jax.ShapeDtypeStruct((half, width), BF),
            jax.ShapeDtypeStruct((half, width), BF),
            jax.ShapeDtypeStruct((count, 2), F32),
        ],
    )(first, second, act, gate, w_in, w_out)


def weight_sums(pre, xs, hidden, cs):
    half, width = xs[0].shape
    tile = min(width, 512)

    def body(pre_ref, xa_ref, xb_ref, hidden_ref, ca_ref, cb_ref, in_ref, down_ref):
        in_ref[...] = both(pre_ref, xa_ref, xb_ref)
        down_ref[...] = both(hidden_ref, ca_ref, cb_ref)

    cut = by_columns(half, tile)
    return call(
        body,
        (width // tile,),
        [whole(pre.shape), cut, cut, whole(hidden.shape), cut, cut],
        [by_columns(pre.shape[0], tile), by_columns(hidden.shape[0], tile)],
        [
            jax.ShapeDtypeStruct((pre.shape[0], width), F32),
            jax.ShapeDtypeStruct((hidden.shape[0], width), F32),
        ],
    )(pre, *xs, hidden, *cs)


def both(left_ref, a_ref, b_ref):
    half = a_ref.shape[0]
    value = jnp.dot(left_ref[:, :half], a_ref[...], preferred_element_type=F32)
    return value + jnp.dot(left_ref[:, half:], b_ref[...], preferred_element_type=F32)


def weight_totals(pre, xs, hidden, cs, in_sum, down_sum, units):
    half, width = xs[0].shape
    tile = min(width, 512)
    padded = hidden.shape[0]
    spare = padded - units

    def body(pre_ref, xa_ref, xb_ref, hidden_ref, ca_ref, cb_ref, in_ref, down_ref, own_ref, hot_ref):
        total = in_ref[...] + both(pre_ref, xa_ref, xb_ref)
        own_ref[:units, :] = total[:units].astype(BF)
        own_ref[units : 2 * units, :] = total[padded : padded + units].astype(BF)
        hot_ref[:spare, :] = total[units:padded].astype(BF)
        hot_ref[spare : 2 * spare, :] = total[padded + units :].astype(BF)
        total = down_ref[...] + both(hidden_ref, ca_ref, cb_ref)
        own_ref[2 * units :, :] = total[:units].astype(BF)
        hot_ref[2 * spare :, :] = total[units:].astype(BF)

    cut = by_columns(half, tile)
    return call(
        body,
        (width // tile,),
        [
            whole(pre.shape), cut, cut, whole(hidden.shape), cut, cut,
            by_columns(2 * padded, tile), by_columns(padded, tile),
        ],
        [by_columns(3 * units, tile), by_columns(3 * spare, tile)],
        [
            jax.ShapeDtypeStruct((3 * units, width), BF),
            jax.ShapeDtypeStruct((3 * spare, width), BF),
        ],
    )(pre, *xs, hidden, *cs, in_sum, down_sum)


def sum_of(*arrays):
    rows, width = arrays[0].shape
    tile = min(rows, 128)

    def body(*refs):
        total = refs[0][...].astype(F32)
        for ref in refs[1:-1]:
            total = total + ref[...].astype(F32)
        refs[-1][...] = total.astype(BF)

    return call(
        body,
        (rows // tile,),
        [by_rows(tile, width)] * len(arrays),
        by_rows(tile, width),
        jax.ShapeDtypeStruct((rows, width), BF),
    )(*arrays)


def halves_of_sum(*arrays, split=()):
    half, width = arrays[0].shape[0] // 2, arrays[0].shape[1]
    tile = min(half, 128)
    tiles = half // tile
    count = len(arrays)

    def body(*refs):
        def run(out_ref, more):
            total = refs[0][...].astype(F32)
            for ref in refs[1:count] + more:
                total = total + ref[...].astype(F32)
            out_ref[...] = total.astype(BF)

        more = refs[count:-2]
        on_both(tiles, run, (refs[-2], more[:1]), (refs[-1], more[1:]))

    shape = jax.ShapeDtypeStruct((half, width), BF)
    ends = [first_rows(tile, width, tiles), second_rows(tile, width, tiles)]
    return call(
        body,
        (2 * tiles,),
        [by_rows(tile, width)] * count + ends[: len(split)],
        ends,
        [shape, shape],
    )(*arrays, *split)


def last_hop(mine, other):
    step = len(chip_bits()) - 1
    return [hop(part, step) for part in halves_of_sum(mine, other)]


def fold(mine, got):
    arrays, split = ((mine,), tuple(got)) if isinstance(got, list) else ((mine, got), ())
    for step in range(len(chip_bits()) - 2, -1, -1):
        mine, other = halves_of_sum(*arrays, split=split)
        arrays, split = (mine, hop(other, step)), ()
    return sum_of(*arrays)


def finish(mine, right, left, hot, is_owner):
    units, width = hot.shape[1:]

    def body(flag_ref, mine_ref, right_ref, left_ref, hot_ref, *out_refs):
        for index, out_ref in enumerate(out_refs):
            rows = slice(index * units, (index + 1) * units)
            total = mine_ref[rows].astype(F32) + right_ref[rows].astype(F32) + left_ref[rows].astype(F32)
            total = jnp.where(flag_ref[0] > 0, hot_ref[index].astype(F32), total)
            out_ref[0] = total.T

    block = whole((3 * units, width))
    return pl.pallas_call(
        body,
        grid=(1,),
        in_specs=[
            pl.BlockSpec(memory_space=pltpu.SMEM), block, block, block,
            pl.BlockSpec((3, units, width), lambda i: (0, 0, 0)),
        ],
        out_specs=[pl.BlockSpec((1, width, units), lambda i: (0, 0, 0))] * 3,
        out_shape=[jax.ShapeDtypeStruct((1, width, units), F32)] * 3,
        compiler_params=pltpu.CompilerParams(vmem_limit_bytes=60 * 1024 * 1024),
    )(is_owner.astype(jnp.int32).reshape(1), mine, right, left, hot)


def hot_pieces(weights, is_owner):
    width, units = weights[0].shape
    part = width // lax.axis_size("dp")
    scalars = jnp.stack([lax.axis_index("dp"), is_owner.astype(jnp.int32)]).astype(jnp.int32)

    def body(scalar_ref, a_ref, b_ref, c_ref, out_ref):
        for index, ref in enumerate((a_ref, b_ref, c_ref)):
            out_ref[index] = ref[...].T

        @pl.when(scalar_ref[1] == 0)
        def _():
            out_ref[...] = jnp.zeros_like(out_ref)

    return pl.pallas_call(
        body,
        grid_spec=pltpu.PrefetchScalarGridSpec(
            num_scalar_prefetch=1,
            grid=(1,),
            in_specs=[pl.BlockSpec((part, units), lambda i, scalars: (scalars[0], 0))] * 3,
            out_specs=pl.BlockSpec((3, units, part), lambda i, scalars: (0, 0, 0)),
        ),
        out_shape=jax.ShapeDtypeStruct((3, units, part), BF),
        cost_estimate=pl.CostEstimate(flops=1000, bytes_accessed=1000, transcendentals=0),
        compiler_params=pltpu.CompilerParams(vmem_limit_bytes=60 * 1024 * 1024),
    )(scalars, *weights)


def widen(weights, hot):
    width, units = weights[0].shape
    spare = hot.shape[1]
    tile = tile_of(width)

    def body(gate_ref, up_ref, down_ref, hot_ref, in_ref, out_ref):
        padded = units + spare
        in_ref[:, :units] = gate_ref[...]
        in_ref[:, units:padded] = hot_ref[0].T
        in_ref[:, padded : padded + units] = up_ref[...]
        in_ref[:, padded + units :] = hot_ref[1].T
        out_ref[:, :units] = down_ref[...]
        out_ref[:, units:] = hot_ref[2].T

    rows = by_rows(tile, units)
    return call(
        body,
        (width // tile,),
        [rows, rows, rows, pl.BlockSpec((3, spare, tile), lambda i: (0, 0, i))],
        [by_rows(tile, 2 * (units + spare)), by_rows(tile, units + spare)],
        [
            jax.ShapeDtypeStruct((width, 2 * (units + spare)), BF),
            jax.ShapeDtypeStruct((width, units + spare), BF),
        ],
    )(*weights, hot)


def per_device(tokens, expert_ids, gates, w_gate, w_up, w_down, cotangent):
    experts, groups = lax.axis_size("expert"), lax.axis_size("dp")
    me, group = lax.axis_index("expert"), lax.axis_index("dp")
    tok_rows, width = tokens.shape
    units = w_gate.shape[2]
    share = units // experts
    last = len(chip_bits()) - 1
    expert_range = jnp.arange(experts, dtype=jnp.int32)
    matches = expert_ids[:, :, None] == expert_range
    hot_expert = jnp.argmax(jnp.sum(matches.astype(jnp.int32), axis=(0, 1))).astype(jnp.int32)
    is_owner = jnp.sum((expert_ids == me).astype(jnp.int32)) == tok_rows
    is_me = ((expert_range == me) & ~is_owner)[:, None]
    is_hot = (expert_range == hot_expert)[:, None]
    routed = jnp.sum(jnp.where(matches, gates[:, :, None], 0.0), axis=1).T
    own = (w_gate[0], w_up[0], w_down[0])
    orders = row_order()
    def halve(value, bit):
        value = value.reshape(3, value.shape[1] // 2, 2, share, width // groups)
        mark = (me // bit) % 2
        other = lax.dynamic_index_in_dim(value, 1 - mark, 2, keepdims=False)
        return lax.dynamic_index_in_dim(value, mark, 2, keepdims=False) + flip(other, bit, bit)

    x_got, c_got, r_got = hop(tokens, 0), hop(cotangent, 0), hop(routed, 0)
    hot = hot_pieces(own, is_owner).reshape(3, experts, share, width // groups)
    hot = halve(hot, 1)
    x_got, c_got, r_got, hot = ends_round(x_got, c_got, r_got, hot)

    x_held, c_held = join(tokens, x_got), join(cotangent, c_got)
    r_held = jnp.concatenate([routed, r_got], axis=1)
    for step in range(1, last):
        x_held = join(x_held, hop(x_held, step))
        c_held = join(c_held, hop(c_held, step))
        r_held = jnp.concatenate([r_held, hop(r_held, step)], axis=1)
    bit = 2
    while bit < experts:
        hot = halve(hot, bit)
        bit *= 2
    r_last = hop(r_held, last)
    x_held, c_held, r_held, r_last, hot = ends_round(x_held, c_held, r_held, r_last, hot)

    x_last, c_last = hop(x_held, last), hop(c_held, last)
    x_other, c_other = swap_core(x_held), swap_core(c_held)
    r_held = jnp.concatenate([r_held, r_last], axis=1)
    r_other = swap_core(r_held)
    half = x_held.shape[0]
    own_gate, hot_gate = (
        [jnp.sum(jnp.where(mask, table, 0.0), axis=0) for table in (r_held, r_other)]
        for mask in (is_me, is_hot)
    )

    def gates_of(part):
        columns = [
            jnp.concatenate([value[part] for value in values]) for values in (own_gate, hot_gate)
        ]
        return jnp.stack(columns).T

    gate_near, gate_far = gates_of(slice(None, half)), gates_of(slice(half, None))
    hot = line_gather(hot.reshape(3 * share, width // groups)).reshape(3, share, width)
    spare = share + -(units + share) % 128
    w_in, w_out = widen(own, jnp.pad(hot, ((0, 0), (0, spare - share), (0, 0))))
    a_near, s_near, m_near, m_near_far = forward(x_held, x_other, gate_near, w_in, w_out, units)
    p_near, t_near, t_near_far, d_near = backward(
        c_held, c_other, a_near, gate_near, w_in, w_out, units
    )
    (
        x_last, c_last, m_near, m_near_far, t_near, t_near_far, d_near, gate_far,
        w_in, w_out, p_near, s_near, x_held, x_other, c_held, c_other,
    ) = ends_round(
        x_last, c_last, m_near, m_near_far, t_near, t_near_far, d_near, gate_far,
        w_in, w_out, p_near, s_near, x_held, x_other, c_held, c_other,
    )

    x_last_other, c_last_other = swap_core(x_last), swap_core(c_last)
    in_near, down_near = weight_sums(p_near, (x_held, x_other), s_near, (c_held, c_other))
    x_last, x_last_other, c_last, c_last_other, m_near, m_near_far, t_near, t_near_far, in_near, down_near = (
        ends_round(
            x_last, x_last_other, c_last, c_last_other, m_near, m_near_far, t_near, t_near_far,
            in_near, down_near,
        )
    )

    m_near_other, t_near_other = swap_core(m_near_far), swap_core(t_near_far)
    a_far, s_far, m_far, m_far_far = forward(x_last, x_last_other, gate_far, w_in, w_out, units)
    m_far_other = swap_core(m_far_far)
    p_far, t_far, t_far_far, d_far = backward(
        c_last, c_last_other, a_far, gate_far, w_in, w_out, units
    )
    t_far_other = swap_core(t_far_far)
    own_grad, hot_grad = weight_totals(
        p_far, (x_last, x_last_other), s_far, (c_last, c_last_other), in_near, down_near, units
    )
    line = LineSum(own_grad)
    right, left = line.sends(1)
    (
        right, left, m_far, m_far_other, t_far, t_far_other, d_far, hot_grad,
        m_near, m_near_other, t_near, t_near_other,
    ) = ends_round(
        right, left, m_far, m_far_other, t_far, t_far_other, d_far, hot_grad,
        m_near, m_near_other, t_near, t_near_other,
    )

    line.send(1, right, left)
    m_got = last_hop(m_far, m_far_other)
    t_far = sum_of(t_far, t_far_other)
    m_near, t_near = sum_of(m_near, m_near_other), sum_of(t_near, t_near_other)
    hot_grad = hot_grad.reshape(3, spare, width)[:, :share].reshape(3 * share, width)
    hot_sum = lax.psum_scatter(hot_grad, "dp", scatter_dimension=1, tiled=True)
    t_far, m_near, t_near, line.right, line.left, *m_got = ends_round(
        t_far, m_near, t_near, line.right, line.left, *m_got
    )

    right, left = line.sends(2)
    right, left, t_far, m_near, *m_got = ends_round(right, left, t_far, m_near, *m_got)
    line.send(2, right, left)
    t_got = hop(t_far, last)
    mixed = fold(m_near, m_got)
    dots = lax.all_gather(jnp.concatenate([d_near, d_far]).T, "expert", axis=0)
    mixed, t_got, dots, hot_sum, line.right, line.left = ends_round(
        mixed, t_got, dots, hot_sum, line.right, line.left
    )

    for step in range(3, groups):
        right, left = line.sends(step)
        right, left, t_near, t_got = ends_round(right, left, t_near, t_got)
        line.send(step, right, left)
    tokens_grad = fold(t_near, t_got)
    hot_all = lax.all_gather(hot_sum.astype(BF), "expert", axis=0)

    my_dots = []
    for source in range(experts):
        order = orders[source % 2]
        place = jnp.array([order.index(r) for r in range(experts)], jnp.int32)
        place = jnp.sum(jnp.where(expert_range == (me ^ source), place, 0))
        my_dots.append(lax.dynamic_slice_in_dim(dots[source], place * tok_rows, tok_rows, 1))
    my_dots = jnp.stack(my_dots)
    hot_dot = jnp.sum(my_dots[:, 1], axis=0)
    own_dot = jnp.sum(jnp.where(matches, my_dots[:, 0].T[:, None, :], 0.0), axis=2)
    gates_grad = jnp.where(expert_ids == hot_expert, hot_dot[:, None], own_dot)

    hot_all = hot_all.reshape(experts, 3, share, width // groups)
    hot_all = jnp.moveaxis(hot_all, 1, 0).reshape(3, units, width // groups)
    grads = finish(line.block(group), line.right, line.left, hot_all, is_owner)
    return (mixed, tokens_grad, gates_grad, *grads)


def solution(mesh):
    rows = P(("dp", "expert"), None)
    weight = P("expert", None, None)
    grad = P("expert", "dp", None)
    return jax.shard_map(
        per_device,
        mesh=mesh,
        in_specs=(rows, rows, rows, weight, weight, weight, rows),
        out_specs=(rows, rows, rows, grad, grad, grad),
        check_vma=False,
    )
```
